128 devices in a mesh: ctx: 32 (over z, x, core), head: 4 (over y).
Axes of the slice: x: 4, y: 4, z: 4, core: 2. Of those that a mesh axis runs over, the one named last changes fastest.
Arguments:
- queries: bfloat16 [16384, 8192], P(('ctx', 'head')), may hold values from -6 to 6
- key_states: bfloat16 [16384, 1024], P(('ctx', 'head')), may hold values from -6 to 6
- value_states: bfloat16 [16384, 1024], P(('ctx', 'head')), may hold values from -6 to 6
- out_grads: bfloat16 [16384, 8192], P(('ctx', 'head')), may hold values from -6 to 6
- doc_blocks: int32 [16], replicated, may hold values from 1 to 12, 128 in all
Outputs:
- attended: bfloat16 [16384, 8192], P('ctx', 'head')
- query_grads: bfloat16 [16384, 8192], P('ctx', 'head')
- key_grads: bfloat16 [16384, 1024], P('ctx', 'head')
- value_grads: bfloat16 [16384, 1024], P('ctx', 'head')
The draws below stay inside these ranges and needn't reach their ends.
Inputs may be any that keep to these rules, and one draw needn't show every extreme that they name: `doc_blocks`: the lengths sum to 128; the longest is exactly 12.
All inputs are finite; a program needn't handle non-finite values.
Results may differ from the reference program's by a relative error of at most 0.012.
The reference program's roundings to bfloat16 on the way (of `rounded` and `dscores`) count: a program that leaves them out, or rounds other values in their place, can miss the bound.
Values may be sent and summed in bfloat16 or wider, within the bound.
A program may use at most 128 MiB of HBM per device.

```python
import math
import jax
import jax.numpy as jnp
import numpy as np
from jax import lax

HQ = 64
HK = 8
DH = 128
BLOCK = 128
NBLK = 128
TOKENS = 16384
MAXDOC = 12
DOCS = 16


def draw_queries(key, part):
    key = jax.random.fold_in(key, 7)
    drawn = jnp.clip(jax.random.normal(key, (TOKENS, HQ * DH), jnp.float32), -6.0, 6.0)
    return drawn.astype(jnp.bfloat16)


def draw_key_states(key, part):
    key = jax.random.fold_in(key, 9)
    drawn = jnp.clip(jax.random.normal(key, (TOKENS, HK * DH), jnp.float32), -6.0, 6.0)
    return drawn.astype(jnp.bfloat16)


def block_levels(stream_key, shape, cuts, least, high):
    factor_of, own = 1.0, jax.random.fold_in(stream_key, 6)
    for position, shards_of in cuts:
        steps = jnp.exp(jax.random.uniform(jax.random.fold_in(own, position), (shards_of,), jnp.float32, least / len(cuts), high / len(cuts)))
        factor_of = factor_of * jnp.repeat(steps, shape[position] // shards_of).reshape([-1 if axis == position else 1 for axis in range(len(shape))])
    return factor_of


def length_profile(amount, total, limit, slope):
    weights = [(1 << 20) // math.isqrt(grade ** slope) + 1 for grade in range(2, amount + 1)]
    surplus, given = total - limit - (amount - 1), [1] * (amount - 1)
    while surplus > 0:
        movable = [i for i in range(amount - 1) if given[i] < limit]
        mass, remaining = sum([weights[i] for i in movable]), surplus
        for i in movable:
            extra = min(limit - given[i], max(1, remaining * weights[i] // mass), surplus)
            given[i] = given[i] + extra
            surplus = surplus - extra
    return np.array([limit] + given)


def ragged_sizes(own_key, count, total, limit, slope):
    if count == 2:
        one = jax.random.randint(own_key, (), max(1, total - limit), min(limit, total - 1) + 1)
        return jnp.stack([one, total - one])
    sizes = jnp.asarray(length_profile(count, total, limit, slope), jnp.int32)
    pairs = (count - 1) // 2
    giver, sink = sizes[1:1 + 2 * pairs:2], sizes[2:2 + 2 * pairs:2]
    slack = jnp.minimum(giver - 1, limit - sink)
    moved = jax.random.randint(jax.random.fold_in(own_key, 1), (pairs,), 0, 1 << 20) % (slack + 1)
    sizes = sizes.at[1:1 + 2 * pairs:2].set(giver - moved).at[2:2 + 2 * pairs:2].set(sink + moved)
    return sizes[jax.random.permutation(jax.random.fold_in(own_key, 2), count)]


def noise(own_key, dims, width, reach, cuts=(), kind=jnp.bfloat16):
    loudness = block_levels(own_key, dims, cuts, -0.22, 0.18) if cuts else 1.0
    values = jax.random.normal(own_key, dims, jnp.float32) * width * loudness
    return jnp.minimum(jnp.maximum(values, -reach), reach).astype(kind)


def setup_inputs(seed: int = 0) -> dict:
    key_list = jax.random.split(jax.random.key(seed), 6)
    return {
        "queries": draw_queries(jax.random.fold_in(key_list[5], 71), 0),
        "key_states": draw_key_states(jax.random.fold_in(key_list[5], 71), 0),
        "value_states": noise(key_list[2], (TOKENS, HK * DH), 1.0, 6.0, ((0, 128),)),
        "out_grads": noise(key_list[3], (TOKENS, HQ * DH), 1.0, 6.0, ((0, 128),)),
        "doc_blocks": ragged_sizes(key_list[4], DOCS, NBLK, MAXDOC, 2).astype(jnp.int32),
    }


MASKED = -1e+30

def reference(queries, key_states, value_states, out_grads, doc_blocks):
    group_size = HQ // HK
    inv_root = 1.0 / math.sqrt(DH)
    doc_ends = jnp.cumsum(doc_blocks).astype(jnp.int32)
    block_ids = jnp.arange(NBLK, dtype=jnp.int32)
    block_doc = lax.optimization_barrier(jnp.sum((doc_ends[None, :] <= block_ids[:, None]).astype(jnp.int32), axis=1)).astype(jnp.int32)
    token_doc = jnp.repeat(block_doc, BLOCK, total_repeat_length=TOKENS).astype(jnp.int32)
    reach_tokens = (MAXDOC - 1) * BLOCK
    window_len = MAXDOC * BLOCK
    pad_keys = jnp.concatenate([jnp.zeros((reach_tokens, HK * DH), key_states.dtype), key_states], axis=0).reshape(reach_tokens + TOKENS, HK, DH)
    pad_values = jnp.concatenate([jnp.zeros((reach_tokens, HK * DH), value_states.dtype), value_states], axis=0).reshape(reach_tokens + TOKENS, HK, DH)
    pad_docs = jnp.concatenate([jnp.full((reach_tokens,), -1, jnp.int32), token_doc]).astype(jnp.int32)
    query_blocks = queries.reshape(NBLK, BLOCK, HK, group_size, DH)
    grad_blocks = out_grads.reshape(NBLK, BLOCK, HK, group_size, DH)
    positions = jnp.arange(BLOCK, dtype=jnp.int32)
    key_places = jnp.arange(window_len, dtype=jnp.int32)

    def one_block(carried, inputs):
        key_grad, value_grad = carried
        block_id, query_block, grad_block = inputs
        window_start = (block_id * BLOCK).astype(jnp.int32)
        key_tile = lax.dynamic_slice_in_dim(pad_keys, window_start, window_len, 0).astype(jnp.float32)
        value_tile = lax.dynamic_slice_in_dim(pad_values, window_start, window_len, 0).astype(jnp.float32)
        doc_tile = lax.dynamic_slice_in_dim(pad_docs, window_start, window_len, 0)
        query_doc = lax.dynamic_slice_in_dim(token_doc, window_start, BLOCK, 0)
        allowed = (doc_tile[None, :] == query_doc[:, None]) & (key_places[None, :] <= positions[:, None] + reach_tokens)
        query_f = query_block.astype(jnp.float32)
        grad_f = grad_block.astype(jnp.float32)
        scores = jnp.einsum('qhgd,khd->hgqk', query_f, key_tile) * inv_root
        scores = jnp.where(allowed, scores, MASKED)
        row_top = lax.optimization_barrier(jnp.max(scores, axis=-1, keepdims=True))
        log_total = row_top + jnp.log(lax.optimization_barrier(jnp.sum(jnp.exp(scores - row_top), axis=-1, keepdims=True)))
        weights = jnp.exp(scores - log_total)
        rounded = lax.optimization_barrier(weights.astype(jnp.bfloat16)).astype(jnp.float32)
        attended = jnp.einsum('hgqk,khd->qhgd', rounded, value_tile).astype(jnp.bfloat16)
        attended_f = lax.optimization_barrier(attended).astype(jnp.float32)
        row_delta = jnp.transpose(lax.optimization_barrier(jnp.sum(grad_f * attended_f, axis=-1)), (1, 2, 0))[..., None]
        dweights = jnp.einsum('qhgd,khd->hgqk', grad_f, value_tile)
        dscores = lax.optimization_barrier((weights * (dweights - row_delta)).astype(jnp.bfloat16)).astype(jnp.float32)
        query_grad = (jnp.einsum('hgqk,khd->qhgd', dscores, key_tile) * inv_root).astype(jnp.bfloat16)
        key_term = jnp.einsum('hgqk,qhgd->khd', dscores, query_f) * inv_root
        value_term = jnp.einsum('hgqk,qhgd->khd', rounded, grad_f)
        key_grad = lax.dynamic_update_slice_in_dim(key_grad, lax.dynamic_slice_in_dim(key_grad, window_start, window_len, 0) + key_term, window_start, 0)
        value_grad = lax.dynamic_update_slice_in_dim(value_grad, lax.dynamic_slice_in_dim(value_grad, window_start, window_len, 0) + value_term, window_start, 0)
        return ((key_grad, value_grad), (attended, query_grad))
    empty_grad = jnp.zeros((reach_tokens + TOKENS, HK, DH), jnp.float32)
    (key_grad, value_grad), (attended, query_grad) = lax.scan(one_block, (empty_grad, empty_grad), (block_ids, query_blocks, grad_blocks))
    return (attended.reshape(TOKENS, HQ * DH), query_grad.reshape(TOKENS, HQ * DH), key_grad[reach_tokens:].reshape(TOKENS, HK * DH).astype(jnp.bfloat16), value_grad[reach_tokens:].reshape(TOKENS, HK * DH).astype(jnp.bfloat16))
```

```python
import math

import jax
import jax.numpy as jnp
from jax import lax
from jax.experimental import pallas as pl
from jax.experimental.pallas import tpu as pltpu
from jax.sharding import PartitionSpec as P

HQ = 64
HK = 8
DH = 128
BLOCK = 128
MAXDOC = 12
DOCS = 16

CTX = 32
HEADS = 4
GROUP = HQ // HK
KV = HK // HEADS
SHARD = 4
SLOTS = 16
SPAN = MAXDOC * BLOCK
QCOLS = GROUP * DH

INV = 1.0 / math.sqrt(DH)
EXP2_SCALE = INV * math.log2(math.e)
MASKED = -1e30

MESH = pl.DeviceIdType.MESH
NN = (((1,), (0,)), ((), ()))
NT = (((1,), (1,)), ((), ()))
TN = (((0,), (0,)), ((), ()))


def dot(a, b, dims):
    return lax.dot_general(a, b, dims, preferred_element_type=jnp.float32)


def rows(first_block, blocks):
    start = first_block * BLOCK
    if not isinstance(first_block, int):
        start = pl.multiple_of(start, BLOCK)
    return pl.ds(start, blocks * BLOCK)


def columns(first, width):
    return pl.ds(pl.multiple_of(first, BLOCK), width)


def kernel(
    docs, q_in, k_in, v_in, g_in, o_out, dq_out, dk_out, dv_out,
    q_buf, g_buf, kv_buf, dk_acc, dv_acc, part, landed, p_buf, ds_buf, gs_buf,
    kv_send, kv_recv, fwd_send, fwd_recv, q_send, q_recv, part_send, part_recv,
):
    c = lax.axis_index("ctx")
    h = lax.axis_index("head")
    parity = lax.rem(c, 2)

    def ctx_at(delta):
        return lax.rem(c + (delta + CTX), CTX)

    def head_at(step):
        return lax.rem(h + step, HEADS)

    barrier = pltpu.get_barrier_semaphore()
    for step in range(1, HEADS):
        pl.semaphore_signal(barrier, inc=1, device_id=(c, head_at(step)), device_id_type=MESH)
    for delta in (-3, -2, -1, 1, 2, 3):
        pl.semaphore_signal(barrier, inc=1, device_id=(ctx_at(delta), h), device_id_type=MESH)
    pl.semaphore_wait(barrier, 9)

    def kv_copy(which, step):
        source = (k_in, v_in)[which]
        peer = head_at(step)
        src = source.at[:, columns(peer * (KV * DH), KV * DH)]
        dst = kv_buf.at[which, rows(12 + h, 1), :]
        if step == 0:
            return pltpu.make_async_copy(src, dst, kv_recv.at[which, 0])
        return pltpu.make_async_remote_copy(
            src, dst, kv_send.at[which, step], kv_recv.at[which, step],
            device_id=(c, peer), device_id_type=MESH,
        )

    def qg_copy(which, group, step):
        source, target = ((q_in, q_buf), (g_in, g_buf))[which]
        peer = head_at(step)
        src = source.at[:, columns(peer * (KV * QCOLS) + group * QCOLS, QCOLS)]
        dst = target.at[h, :, pl.ds(group * QCOLS, QCOLS)]
        if step == 0:
            return pltpu.make_async_copy(src, dst, q_recv.at[which, group, 0])
        return pltpu.make_async_remote_copy(
            src, dst, q_send.at[which, group, step], q_recv.at[which, group, step],
            device_id=(c, peer), device_id_type=MESH,
        )

    def shard_copy(index, src_block, dst_block, blocks, delta):
        return pltpu.make_async_remote_copy(
            kv_buf.at[:, rows(src_block, blocks), :],
            kv_buf.at[:, rows(dst_block, blocks), :],
            fwd_send.at[index], fwd_recv.at[index],
            device_id=(ctx_at(delta), h), device_id_type=MESH,
        )

    own_next = lambda: shard_copy(1, 12, 8, 4, 1)
    own_two = lambda: shard_copy(2, 12, 4, 4, 2)
    own_three = lambda: shard_copy(3, 13, 1, 3, 3)
    pass_next = lambda: shard_copy(3, 5, 1, 3, 1)
    pass_back = lambda: shard_copy(1, 4, 8, 4, -1)

    for step in (1, 3, 2, 0):
        for which in range(2):
            kv_copy(which, step).start()
    for group in range(KV):
        for step in (0, 1, 3, 2):
            for which in range(2):
                qg_copy(which, group, step).start()

    dk_acc[...] = jnp.zeros_like(dk_acc)
    dv_acc[...] = jnp.zeros_like(dv_acc)

    firsts = []
    for b in range(SHARD):
        block = c * SHARD + b
        begin = jnp.int32(0)
        first = jnp.int32(0)
        for d in range(DOCS):
            end = begin + docs[d]
            first = jnp.where((block >= begin) & (block < end), begin, first)
            begin = end
        firsts.append(first - (block - (MAXDOC - 1)))

    for step in range(HEADS):
        for which in range(2):
            if step == 0:
                kv_copy(which, step).wait()
            else:
                kv_copy(which, step).wait_recv()

    own_two().start()

    @pl.when(parity == 0)
    def _():
        own_next().start()

    @pl.when(parity == 1)
    def _():
        own_three().start()

    own_two().wait_recv()

    @pl.when(parity == 0)
    def _():
        pass_next().start()

    @pl.when(parity == 1)
    def _():
        pass_back().start()

    own_next().wait_recv()
    own_three().wait_recv()

    def part_copy(group, delta):
        blocks = 3 if delta == 3 else 4
        source = 1 if delta == 3 else 12 - 4 * delta
        target = 1 if delta == 3 else 0
        return pltpu.make_async_remote_copy(
            part.at[:, group, rows(source, blocks), :],
            landed.at[delta - 1, :, group, rows(target, blocks), :],
            part_send.at[group, delta - 1], part_recv.at[group, delta - 1],
            device_id=(ctx_at(-delta), h), device_id_type=MESH,
        )

    tri = lax.broadcasted_iota(jnp.int32, (QCOLS, BLOCK), 1) <= (
        lax.broadcasted_iota(jnp.int32, (QCOLS, BLOCK), 0) & (BLOCK - 1)
    )

    def unit(index, _):
        group = index // HEADS
        step = lax.rem(index, HEADS)
        b = lax.rem(h + HEADS - step, HEADS)
        for which, buf in ((0, q_buf), (1, g_buf)):
            here = buf.at[b, :, columns(group * QCOLS, QCOLS)]
            pltpu.make_async_copy(here, here, q_recv.at[which, group, step]).wait()
        low = firsts[0]
        for other in range(1, SHARD):
            low = jnp.where(b == other, firsts[other], low)
        window = pl.ds(pl.multiple_of((b + 1) * BLOCK, BLOCK), SPAN)
        features = columns(group * DH, DH)
        k = kv_buf[0, window, features]
        v = kv_buf[1, window, features]
        heads = [columns(group * QCOLS + i * DH, DH) for i in range(GROUP)]
        q = jnp.concatenate([q_buf[b, :, at] for at in heads], 0)
        grad = jnp.concatenate([g_buf[b, :, at] for at in heads], 0)
        s = dot(q, k, NT)
        tiles = []
        for j in range(MAXDOC):
            tile = s[:, j * BLOCK : (j + 1) * BLOCK]
            keep = tri if j == MAXDOC - 1 else low <= j
            tiles.append(jnp.where(keep, tile, MASKED))
        top = tiles[0]
        for tile in tiles[1:]:
            top = jnp.maximum(top, tile)
        top = jnp.max(top, axis=1, keepdims=True) * EXP2_SCALE
        total = None
        weights = []
        for tile in tiles:
            p = jnp.exp2(tile * EXP2_SCALE - top)
            total = p if total is None else total + p
            weights.append(p.astype(jnp.bfloat16))
        scale = 1.0 / jnp.sum(total, axis=1, keepdims=True)
        p_all = jnp.concatenate(weights, 1)
        p_buf[...] = p_all
        out = (dot(p_all, v, NN) * scale).astype(jnp.bfloat16)
        grad_f = grad.astype(jnp.float32)
        delta = jnp.sum(grad_f * out.astype(jnp.float32), axis=1, keepdims=True) * scale
        grad_s = (grad_f * scale).astype(jnp.bfloat16)
        gs_buf[...] = grad_s
        dp = dot(grad_s, v, NT)
        terms = []
        for j in range(MAXDOC):
            inner = dp[:, j * BLOCK : (j + 1) * BLOCK] - delta
            terms.append((weights[j].astype(jnp.float32) * inner).astype(jnp.bfloat16))
        ds = jnp.concatenate(terms, 1)
        ds_buf[...] = ds
        dq = (dot(ds, k, NN) * INV).astype(jnp.bfloat16)
        for i, at in enumerate(heads):
            o_out[b, :, at] = out[i * BLOCK : (i + 1) * BLOCK]
            dq_out[b, :, at] = dq[i * BLOCK : (i + 1) * BLOCK]
        dv_acc[group, window, :] += dot(p_buf[...], gs_buf[...], TN)
        dk_acc[group, window, :] += dot(ds_buf[...], q, TN)

        @pl.when(step == HEADS - 1)
        def _():
            part[0, group] = (dk_acc[group, : 12 * BLOCK, :] * INV).astype(jnp.bfloat16)
            part[1, group] = dv_acc[group, : 12 * BLOCK, :].astype(jnp.bfloat16)
            for delta in (1, 2, 3):
                part_copy(group, delta).start()

        return 0

    lax.fori_loop(0, KV * HEADS, unit, 0)

    for group in range(KV):
        for delta in (1, 2, 3):
            part_copy(group, delta).wait_recv()
        lanes = slice(group * DH, (group + 1) * DH)
        for which, acc, out in ((0, dk_acc, dk_out), (1, dv_acc, dv_out)):
            for block in range(SHARD):
                at = slice(block * BLOCK, (block + 1) * BLOCK)
                total = acc[group, (12 + block) * BLOCK : (13 + block) * BLOCK, :]
                if which == 0:
                    total = total * INV
                for delta in (1, 2, 3):
                    if delta < 3 or block > 0:
                        total = total + landed[delta - 1, which, group, at, :].astype(jnp.float32)
                out[at, lanes] = total.astype(jnp.bfloat16)

    for step in range(1, HEADS):
        for which in range(2):
            kv_copy(which, step).wait_send()
            for group in range(KV):
                qg_copy(which, group, step).wait_send()
    own_two().wait_send()

    @pl.when(parity == 0)
    def _():
        own_next().wait_send()
        pass_next().wait_send()

    @pl.when(parity == 1)
    def _():
        own_three().wait_send()
        pass_back().wait_send()

    for group in range(KV):
        for delta in (1, 2, 3):
            part_copy(group, delta).wait_send()


def shards(queries, key_states, value_states, out_grads, doc_blocks):
    bf16, f32 = jnp.bfloat16, jnp.float32
    anywhere = pl.BlockSpec(memory_space=pl.ANY)
    vmem = pl.BlockSpec(memory_space=pltpu.VMEM)
    dma = pltpu.SemaphoreType.DMA
    tokens = SHARD * BLOCK
    out, dq, dk, dv = pl.pallas_call(
        kernel,
        out_shape=[
            jax.ShapeDtypeStruct((SHARD, BLOCK, KV * QCOLS), bf16),
            jax.ShapeDtypeStruct((SHARD, BLOCK, KV * QCOLS), bf16),
            jax.ShapeDtypeStruct((tokens, KV * DH), bf16),
            jax.ShapeDtypeStruct((tokens, KV * DH), bf16),
        ],
        in_specs=[pl.BlockSpec(memory_space=pltpu.SMEM)] + [anywhere] * 4,
        out_specs=[vmem] * 4,
        scratch_shapes=[
            pltpu.VMEM((SHARD, BLOCK, KV * QCOLS), bf16),
            pltpu.VMEM((SHARD, BLOCK, KV * QCOLS), bf16),
            pltpu.VMEM((2, SLOTS * BLOCK, KV * DH), bf16),
            pltpu.VMEM((KV, SLOTS * BLOCK, DH), f32),
            pltpu.VMEM((KV, SLOTS * BLOCK, DH), f32),
            pltpu.VMEM((2, KV, 12 * BLOCK, DH), bf16),
            pltpu.VMEM((3, 2, KV, tokens, DH), bf16),
            pltpu.VMEM((QCOLS, SPAN), bf16),
            pltpu.VMEM((QCOLS, SPAN), bf16),
            pltpu.VMEM((QCOLS, DH), bf16),
            dma((2, HEADS)), dma((2, HEADS)),
            dma((4,)), dma((4,)),
            dma((2, KV, HEADS)), dma((2, KV, HEADS)),
            dma((KV, 3)), dma((KV, 3)),
        ],
        compiler_params=pltpu.CompilerParams(
            collective_id=0, has_side_effects=True, vmem_limit_bytes=60 * 2**20
        ),
        name="attention",
    )(doc_blocks, queries, key_states, value_states, out_grads)
    width = KV * QCOLS
    return out.reshape(tokens, width), dq.reshape(tokens, width), dk, dv


def solution(mesh):
    entry = P(("ctx", "head"), None)
    return jax.shard_map(
        shards,
        mesh=mesh,
        in_specs=(entry, entry, entry, entry, P()),
        out_specs=(P("ctx", "head"),) * 4,
        check_vma=False,
    )
```

```python
import math

import jax
import jax.numpy as jnp
from jax import lax
from jax.experimental import pallas as pl
from jax.experimental.pallas import tpu as pltpu
from jax.sharding import PartitionSpec as P

HQ = 64
HK = 8
DH = 128
BLOCK = 128
MAXDOC = 12
DOCS = 16

CTX = 32
HEADS = 4
GROUP = HQ // HK
KV = HK // HEADS
SHARD = 4
SLOTS = 16
SPAN = MAXDOC * BLOCK
QCOLS = GROUP * DH
PIECES = ((1, 2, 3), (3, 1, 3), (4, 4, 2), (8, 4, 1))

INV = 1.0 / math.sqrt(DH)
EXP2_SCALE = INV * math.log2(math.e)
MASKED = -1e30

MESH = pl.DeviceIdType.MESH
NN = (((1,), (0,)), ((), ()))
NT = (((1,), (1,)), ((), ()))
TN = (((0,), (0,)), ((), ()))


def dot(a, b, dims):
    return lax.dot_general(a, b, dims, preferred_element_type=jnp.float32)


def rows(first_block, blocks):
    start = first_block * BLOCK
    if not isinstance(first_block, int):
        start = pl.multiple_of(start, BLOCK)
    return pl.ds(start, blocks * BLOCK)


def columns(first, width):
    return pl.ds(pl.multiple_of(first, BLOCK), width)


def kernel(
    docs, q_in, k_in, v_in, g_in, o_out, dq_out, dk_out, dv_out,
    q_buf, g_buf, kv_buf, dk_acc, dv_acc, part, landed, p_buf, ds_buf, gs_buf,
    kv_send, kv_recv, fwd_send, fwd_recv, q_send, q_recv, part_send, part_recv,
):
    c = lax.axis_index("ctx")
    h = lax.axis_index("head")
    parity = lax.rem(c, 2)

    def ctx_at(delta):
        return lax.rem(c + (delta + CTX), CTX)

    def head_at(step):
        return lax.rem(h + step, HEADS)

    barrier = pltpu.get_barrier_semaphore()
    for step in range(1, HEADS):
        pl.semaphore_signal(barrier, inc=1, device_id=(c, head_at(step)), device_id_type=MESH)
    for delta in (-3, -2, -1, 1, 2, 3):
        pl.semaphore_signal(barrier, inc=1, device_id=(ctx_at(delta), h), device_id_type=MESH)
    pl.semaphore_wait(barrier, 9)

    def kv_copy(which, step):
        source = (k_in, v_in)[which]
        peer = head_at(step)
        src = source.at[:, columns(peer * (KV * DH), KV * DH)]
        dst = kv_buf.at[which, rows(12 + h, 1), :]
        if step == 0:
            return pltpu.make_async_copy(src, dst, kv_recv.at[which, 0])
        return pltpu.make_async_remote_copy(
            src, dst, kv_send.at[which, step], kv_recv.at[which, step],
            device_id=(c, peer), device_id_type=MESH,
        )

    def qg_copy(which, group, step):
        source, target = ((q_in, q_buf), (g_in, g_buf))[which]
        peer = head_at(step)
        src = source.at[:, columns(peer * (KV * QCOLS) + group * QCOLS, QCOLS)]
        dst = target.at[h, :, pl.ds(group * QCOLS, QCOLS)]
        if step == 0:
            return pltpu.make_async_copy(src, dst, q_recv.at[which, group, 0])
        return pltpu.make_async_remote_copy(
            src, dst, q_send.at[which, group, step], q_recv.at[which, group, step],
            device_id=(c, peer), device_id_type=MESH,
        )

    def block_copy(kind, step, src_slot, dst_slot, delta):
        b = lax.rem(h + HEADS - step, HEADS)
        return pltpu.make_async_remote_copy(
            kv_buf.at[:, rows(src_slot + b, 1), :],
            kv_buf.at[:, rows(dst_slot + b, 1), :],
            fwd_send.at[kind, step], fwd_recv.at[kind, step],
            device_id=(ctx_at(delta), h), device_id_type=MESH,
        )

    to_sibling = lambda step: block_copy(0, step, 12, 8, 1)
    back_sibling = lambda step: block_copy(0, step, 4, 8, -1)
    to_second = lambda step: block_copy(1, step, 12, 4, 2)
    pass_third = lambda step: block_copy(2, step, 4, 0, 1)

    for step in (1, 3, 2, 0):
        for which in range(2):
            kv_copy(which, step).start()
    for group in range(KV):
        for step in (0, 1, 3, 2):
            for which in range(2):
                qg_copy(which, group, step).start()

    dk_acc[...] = jnp.zeros_like(dk_acc)
    dv_acc[...] = jnp.zeros_like(dv_acc)

    firsts = []
    for b in range(SHARD):
        block = c * SHARD + b
        begin = jnp.int32(0)
        first = jnp.int32(0)
        for d in range(DOCS):
            end = begin + docs[d]
            first = jnp.where((block >= begin) & (block < end), begin, first)
            begin = end
        firsts.append(first - (block - (MAXDOC - 1)))

    def send_own(step):
        for which in range(2):
            if step == 0:
                kv_copy(which, step).wait()
            else:
                kv_copy(which, step).wait_recv()
        to_second(step).start()

        @pl.when(parity == 0)
        def _():
            to_sibling(step).start()

    def send_on(step):
        to_second(step).wait_recv()

        @pl.when(h != step)
        def _():
            pass_third(step).start()

        @pl.when(parity == 1)
        def _():
            back_sibling(step).start()

    send_own(0)
    send_own(1)
    send_on(0)
    send_own(3)
    send_on(1)
    send_own(2)
    send_on(3)
    send_on(2)
    for step in range(HEADS):
        to_sibling(step).wait_recv()

        @pl.when(h != step)
        def _():
            pass_third(step).wait_recv()

    def part_copy(which, group, piece):
        first, blocks, delta = PIECES[piece]
        return pltpu.make_async_remote_copy(
            part.at[which, group, :, pl.ds(first * BLOCK, blocks * BLOCK)],
            landed.at[which, group, delta - 1, :, pl.ds(first % SHARD * BLOCK, blocks * BLOCK)],
            part_send.at[which, group, piece], part_recv.at[which, group, piece],
            device_id=(ctx_at(-delta), h), device_id_type=MESH,
        )

    def send_parts(which, group, pieces):
        for piece in pieces:
            first, blocks, _ = PIECES[piece]
            lanes = slice(first * BLOCK, (first + blocks) * BLOCK)
            total = (dk_acc, dv_acc)[which][group, :, lanes]
            if which == 0:
                total = total * INV
            part[which, group, :, lanes] = total.astype(jnp.bfloat16)
            part_copy(which, group, piece).start()

    tri = lax.broadcasted_iota(jnp.int32, (QCOLS, BLOCK), 1) <= (
        lax.broadcasted_iota(jnp.int32, (QCOLS, BLOCK), 0) & (BLOCK - 1)
    )

    def unit(index, _, last=False):
        early = 1 - (index + 6) // 8
        group = early * index + (1 - early) * ((index + 1) // 3 - 1)
        turn = lax.rem(index + 1, 3)
        usual = 1 + lax.rem(2 * turn, 3)
        inner = (h * (3 - h)) // 2
        ending = (1 - inner) * (3 - turn) + inner * ((h - 1) * (1 + turn) + (2 - h) * usual)
        step = (1 - early) * ((1 - group) * usual + group * ending)
        b = lax.rem(h + HEADS - step, HEADS)
        for which, buf in ((0, q_buf), (1, g_buf)):
            here = buf.at[b, :, columns(group * QCOLS, QCOLS)]
            pltpu.make_async_copy(here, here, q_recv.at[which, group, step]).wait()
        low = firsts[0]
        for other in range(1, SHARD):
            low = jnp.where(b == other, firsts[other], low)
        window = pl.ds(pl.multiple_of((b + 1) * BLOCK, BLOCK), SPAN)
        features = columns(group * DH, DH)
        k = kv_buf[0, window, features]
        v = kv_buf[1, window, features]
        heads = [columns(group * QCOLS + i * DH, DH) for i in range(GROUP)]
        q = jnp.concatenate([q_buf[b, :, at] for at in heads], 0)
        grad = jnp.concatenate([g_buf[b, :, at] for at in heads], 0)
        s = dot(q, k, NT)
        tiles = []
        for j in range(MAXDOC):
            tile = s[:, j * BLOCK : (j + 1) * BLOCK]
            keep = tri if j == MAXDOC - 1 else low <= j
            tiles.append(jnp.where(keep, tile, MASKED))
        top = tiles[0]
        for tile in tiles[1:]:
            top = jnp.maximum(top, tile)
        top = jnp.max(top, axis=1, keepdims=True) * EXP2_SCALE
        total = None
        weights = []
        for tile in tiles:
            p = jnp.exp2(tile * EXP2_SCALE - top)
            total = p if total is None else total + p
            weights.append(p.astype(jnp.bfloat16))
        scale = 1.0 / jnp.sum(total, axis=1, keepdims=True)
        p_all = jnp.concatenate(weights, 1)
        p_buf[...] = p_all
        out = (dot(v.T, p_all.T, NN).T * scale).astype(jnp.bfloat16)
        grad_f = grad.astype(jnp.float32)
        delta = jnp.sum(grad_f * out.astype(jnp.float32), axis=1, keepdims=True) * scale
        grad_s = (grad_f * scale).astype(jnp.bfloat16)
        gs_buf[...] = grad_s
        for i, at in enumerate(heads):
            o_out[b, :, at] = out[i * BLOCK : (i + 1) * BLOCK]
        if last:
            dv_acc[group, :, window] += dot(gs_buf[...], p_buf[...], TN)
            send_parts(1, 1, (2, 1, 3))
        dp = dot(grad_s, v, NT)
        terms = []
        for j in range(MAXDOC):
            inner = dp[:, j * BLOCK : (j + 1) * BLOCK] - delta
            terms.append((weights[j].astype(jnp.float32) * inner).astype(jnp.bfloat16))
        ds = jnp.concatenate(terms, 1)
        ds_buf[...] = ds
        if last:
            dk_acc[group, :, window] += dot(q, ds_buf[...], TN)
            send_parts(0, 1, (2, 1, 3))
        dq = (dot(ds, k, NN) * INV).astype(jnp.bfloat16)
        for i, at in enumerate(heads):
            dq_out[b, :, at] = dq[i * BLOCK : (i + 1) * BLOCK]
        if last:
            return
        dv_acc[group, :, window] += dot(gs_buf[...], p_buf[...], TN)
        dk_acc[group, :, window] += dot(q, ds_buf[...], TN)

        @pl.when(index == HEADS)
        def _():
            for which in (1, 0):
                send_parts(which, 0, (0, 1, 2, 3))

        return 0

    lax.fori_loop(0, KV * HEADS - 1, unit, 0)
    send_parts(1, 1, (0,))
    send_parts(0, 1, (0,))
    unit(KV * HEADS - 1, 0, last=True)

    for group in range(KV):
        for which in range(2):
            for piece in range(len(PIECES)):
                part_copy(which, group, piece).wait_recv()
        lanes = slice(group * DH, (group + 1) * DH)
        for which, acc, out in ((0, dk_acc, dk_out), (1, dv_acc, dv_out)):
            for block in range(SHARD):
                at = slice(block * BLOCK, (block + 1) * BLOCK)
                total = acc[group, :, (12 + block) * BLOCK : (13 + block) * BLOCK]
                if which == 0:
                    total = total * INV
                for delta in (1, 2, 3):
                    if delta < 3 or block > 0:
                        total = total + landed[which, group, delta - 1, :, at].astype(jnp.float32)
                out[at, lanes] = total.T.astype(jnp.bfloat16)

    for step in range(1, HEADS):
        for which in range(2):
            kv_copy(which, step).wait_send()
            for group in range(KV):
                qg_copy(which, group, step).wait_send()
    for step in range(HEADS):
        to_second(step).wait_send()

        @pl.when(h != step)
        def _():
            pass_third(step).wait_send()

        to_sibling(step).wait_send()

    for group in range(KV):
        for which in range(2):
            for piece in range(len(PIECES)):
                part_copy(which, group, piece).wait_send()


def shards(queries, key_states, value_states, out_grads, doc_blocks):
    bf16, f32 = jnp.bfloat16, jnp.float32
    anywhere = pl.BlockSpec(memory_space=pl.ANY)
    vmem = pl.BlockSpec(memory_space=pltpu.VMEM)
    dma = pltpu.SemaphoreType.DMA
    tokens = SHARD * BLOCK
    out, dq, dk, dv = pl.pallas_call(
        kernel,
        out_shape=[
            pltpu.VMEM((SHARD, BLOCK, KV * QCOLS), bf16),
            pltpu.VMEM((SHARD, BLOCK, KV * QCOLS), bf16),
            pltpu.VMEM((tokens, KV * DH), bf16),
            pltpu.VMEM((tokens, KV * DH), bf16),
        ],
        in_specs=[pl.BlockSpec(memory_space=pltpu.SMEM)] + [anywhere] * 4,
        out_specs=[vmem] * 4,
        scratch_shapes=[
            pltpu.VMEM((SHARD, BLOCK, KV * QCOLS), bf16),
            pltpu.VMEM((SHARD, BLOCK, KV * QCOLS), bf16),
            pltpu.VMEM((2, SLOTS * BLOCK, KV * DH), bf16),
            pltpu.VMEM((KV, DH, SLOTS * BLOCK), f32),
            pltpu.VMEM((KV, DH, SLOTS * BLOCK), f32),
            pltpu.VMEM((2, KV, DH, 12 * BLOCK), bf16),
            pltpu.VMEM((2, KV, 3, DH, tokens), bf16),
            pltpu.VMEM((QCOLS, SPAN), bf16),
            pltpu.VMEM((QCOLS, SPAN), bf16),
            pltpu.VMEM((QCOLS, DH), bf16),
            dma((2, HEADS)), dma((2, HEADS)),
            dma((3, HEADS)), dma((3, HEADS)),
            dma((2, KV, HEADS)), dma((2, KV, HEADS)),
            dma((2, KV, 4)), dma((2, KV, 4)),
        ],
        compiler_params=pltpu.CompilerParams(
            collective_id=0, has_side_effects=True, vmem_limit_bytes=58 * 2**20
        ),
        name="attention",
    )(doc_blocks, queries, key_states, value_states, out_grads)
    width = KV * QCOLS
    return out.reshape(tokens, width), dq.reshape(tokens, width), dk, dv


def solution(mesh):
    entry = P(("ctx", "head"), None)
    return jax.shard_map(
        shards,
        mesh=mesh,
        in_specs=(entry, entry, entry, entry, P()),
        out_specs=(P("ctx", "head"),) * 4,
        check_vma=False,
    )
```

```python
import math

import jax
import jax.numpy as jnp
from jax import lax
from jax.experimental import pallas as pl
from jax.experimental.pallas import tpu as pltpu
from jax.sharding import PartitionSpec as P

HQ = 64
HK = 8
DH = 128
BLOCK = 128
MAXDOC = 12
DOCS = 16

CTX = 32
HEADS = 4
GROUP = HQ // HK
KV = HK // HEADS
SHARD = 4
SLOTS = 16
SPAN = MAXDOC * BLOCK
QCOLS = GROUP * DH
PIECES = ((1, 2, 3), (3, 1, 3), (4, 4, 2), (8, 4, 1))

INV = 1.0 / math.sqrt(DH)
EXP2_SCALE = INV * math.log2(math.e)
MASKED = -1e30

MESH = pl.DeviceIdType.MESH
NN = (((1,), (0,)), ((), ()))
NT = (((1,), (1,)), ((), ()))
TN = (((0,), (0,)), ((), ()))


def dot(a, b, dims):
    return lax.dot_general(a, b, dims, preferred_element_type=jnp.float32)


def rows(first_block, blocks):
    start = first_block * BLOCK
    if not isinstance(first_block, int):
        start = pl.multiple_of(start, BLOCK)
    return pl.ds(start, blocks * BLOCK)


def columns(first, width):
    return pl.ds(pl.multiple_of(first, BLOCK), width)


def kernel(
    docs, q_in, k_in, v_in, g_in, o_out, dq_out, dk_out, dv_out,
    q_buf, g_buf, kv_buf, dk_acc, dv_acc, part, landed, p_buf, ds_buf, gs_buf,
    kv_send, kv_recv, fwd_send, fwd_recv, q_send, q_recv, part_send, part_recv,
):
    c = lax.axis_index("ctx")
    h = lax.axis_index("head")
    parity = lax.rem(c, 2)

    def ctx_at(delta):
        return lax.rem(c + (delta + CTX), CTX)

    def head_at(step):
        return lax.rem(h + step, HEADS)

    barrier = pltpu.get_barrier_semaphore()
    for step in range(1, HEADS):
        pl.semaphore_signal(barrier, inc=1, device_id=(c, head_at(step)), device_id_type=MESH)
    for delta in (-3, -2, -1, 1, 2, 3):
        pl.semaphore_signal(barrier, inc=1, device_id=(ctx_at(delta), h), device_id_type=MESH)
    pl.semaphore_wait(barrier, 9)

    def kv_copy(which, step):
        source = (k_in, v_in)[which]
        peer = head_at(step)
        src = source.at[:, columns(peer * (KV * DH), KV * DH)]
        dst = kv_buf.at[which, rows(12 + h, 1), :]
        if step == 0:
            return pltpu.make_async_copy(src, dst, kv_recv.at[which, 0])
        return pltpu.make_async_remote_copy(
            src, dst, kv_send.at[which, step], kv_recv.at[which, step],
            device_id=(c, peer), device_id_type=MESH,
        )

    def qg_copy(which, group, step):
        source, target = ((q_in, q_buf), (g_in, g_buf))[which]
        peer = head_at(step)
        src = source.at[:, columns(peer * (KV * QCOLS) + group * QCOLS, QCOLS)]
        dst = target.at[h, :, pl.ds(group * QCOLS, QCOLS)]
        if step == 0:
            return pltpu.make_async_copy(src, dst, q_recv.at[which, group, 0])
        return pltpu.make_async_remote_copy(
            src, dst, q_send.at[which, group, step], q_recv.at[which, group, step],
            device_id=(c, peer), device_id_type=MESH,
        )

    def block_copy(kind, step, src_slot, dst_slot, delta):
        b = lax.rem(h + HEADS - step, HEADS)
        return pltpu.make_async_remote_copy(
            kv_buf.at[:, rows(src_slot + b, 1), :],
            kv_buf.at[:, rows(dst_slot + b, 1), :],
            fwd_send.at[kind, step], fwd_recv.at[kind, step],
            device_id=(ctx_at(delta), h), device_id_type=MESH,
        )

    to_sibling = lambda step: block_copy(0, step, 12, 8, 1)
    back_sibling = lambda step: block_copy(0, step, 4, 8, -1)
    to_second = lambda step: block_copy(1, step, 12, 4, 2)
    pass_third = lambda step: block_copy(2, step, 4, 0, 1)

    for step in (1, 3, 2, 0):
        for which in range(2):
            kv_copy(which, step).start()
    for group in range(KV):
        for step in (0, 1, 3, 2):
            for which in range(2):
                qg_copy(which, group, step).start()

    dk_acc[...] = jnp.zeros_like(dk_acc)
    dv_acc[...] = jnp.zeros_like(dv_acc)

    firsts = []
    for b in range(SHARD):
        block = c * SHARD + b
        begin = jnp.int32(0)
        first = jnp.int32(0)
        for d in range(DOCS):
            end = begin + docs[d]
            first = jnp.where((block >= begin) & (block < end), begin, first)
            begin = end
        firsts.append(first - (block - (MAXDOC - 1)))

    def send_own(step):
        for which in range(2):
            if step == 0:
                kv_copy(which, step).wait()
            else:
                kv_copy(which, step).wait_recv()
        to_second(step).start()

        @pl.when(parity == 0)
        def _():
            to_sibling(step).start()

    def send_on(step):
        to_second(step).wait_recv()

        @pl.when(h != step)
        def _():
            pass_third(step).start()

        @pl.when(parity == 1)
        def _():
            back_sibling(step).start()

    send_own(0)
    send_own(1)
    send_on(0)
    send_own(3)
    send_on(1)
    send_own(2)
    send_on(3)
    send_on(2)
    for step in range(HEADS):
        to_sibling(step).wait_recv()

        @pl.when(h != step)
        def _():
            pass_third(step).wait_recv()

    def part_copy(which, group, piece):
        first, blocks, delta = PIECES[piece]
        return pltpu.make_async_remote_copy(
            part.at[which, group, :, pl.ds(first * BLOCK, blocks * BLOCK)],
            landed.at[which, group, delta - 1, :, pl.ds(first % SHARD * BLOCK, blocks * BLOCK)],
            part_send.at[which, group, piece], part_recv.at[which, group, piece],
            device_id=(ctx_at(-delta), h), device_id_type=MESH,
        )

    def send_parts(which, group, pieces):
        for piece in pieces:
            first, blocks, _ = PIECES[piece]
            lanes = slice(first * BLOCK, (first + blocks) * BLOCK)
            total = (dk_acc, dv_acc)[which][group, :, lanes]
            if which == 0:
                total = total * INV
            part[which, group, :, lanes] = total.astype(jnp.bfloat16)
            part_copy(which, group, piece).start()

    tri = lax.broadcasted_iota(jnp.int32, (QCOLS, BLOCK), 1) <= (
        lax.broadcasted_iota(jnp.int32, (QCOLS, BLOCK), 0) & (BLOCK - 1)
    )

    def unit(index, _, last=False):
        early = 1 - (index + 6) // 8
        group = early * index + (1 - early) * ((index + 1) // 3 - 1)
        turn = lax.rem(index + 1, 3)
        usual = 1 + lax.rem(2 * turn, 3)
        inner = (h * (3 - h)) // 2
        ending = (1 - inner) * (3 - turn) + inner * ((h - 1) * (1 + turn) + (2 - h) * usual)
        step = (1 - early) * ending
        b = lax.rem(h + HEADS - step, HEADS)
        for which, buf in ((0, q_buf), (1, g_buf)):
            here = buf.at[b, :, columns(group * QCOLS, QCOLS)]
            pltpu.make_async_copy(here, here, q_recv.at[which, group, step]).wait()
        low = firsts[0]
        for other in range(1, SHARD):
            low = jnp.where(b == other, firsts[other], low)
        window = pl.ds(pl.multiple_of((b + 1) * BLOCK, BLOCK), SPAN)
        features = columns(group * DH, DH)
        k = kv_buf[0, window, features]
        v = kv_buf[1, window, features]
        heads = [columns(group * QCOLS + i * DH, DH) for i in range(GROUP)]
        q = jnp.concatenate([q_buf[b, :, at] for at in heads], 0)
        grad = jnp.concatenate([g_buf[b, :, at] for at in heads], 0)
        s = dot(q, k, NT)
        tiles = []
        for j in range(MAXDOC):
            tile = s[:, j * BLOCK : (j + 1) * BLOCK]
            keep = tri if j == MAXDOC - 1 else low <= j
            tiles.append(jnp.where(keep, tile, MASKED))
        top = tiles[0]
        for tile in tiles[1:]:
            top = jnp.maximum(top, tile)
        top = jnp.max(top, axis=1, keepdims=True) * EXP2_SCALE
        total = None
        weights = []
        for tile in tiles:
            p = jnp.exp2(tile * EXP2_SCALE - top)
            total = p if total is None else total + p
            weights.append(p.astype(jnp.bfloat16))
        scale = 1.0 / jnp.sum(total, axis=1, keepdims=True)
        p_all = jnp.concatenate(weights, 1)
        p_buf[...] = p_all
        out = (dot(v.T, p_all.T, NN).T * scale).astype(jnp.bfloat16)
        grad_f = grad.astype(jnp.float32)
        delta = jnp.sum(grad_f * out.astype(jnp.float32), axis=1, keepdims=True) * scale
        grad_s = (grad_f * scale).astype(jnp.bfloat16)
        gs_buf[...] = grad_s
        for i, at in enumerate(heads):
            o_out[b, :, at] = out[i * BLOCK : (i + 1) * BLOCK]
        if last:
            dv_acc[group, :, window] += dot(gs_buf[...], p_buf[...], TN)
            send_parts(1, 1, (2, 1, 3))
        dp = dot(grad_s, v, NT)
        terms = []
        for j in range(MAXDOC):
            inner = dp[:, j * BLOCK : (j + 1) * BLOCK] - delta
            terms.append((weights[j].astype(jnp.float32) * inner).astype(jnp.bfloat16))
        ds = jnp.concatenate(terms, 1)
        ds_buf[...] = ds
        if last:
            dk_acc[group, :, window] += dot(q, ds_buf[...], TN)
            send_parts(0, 1, (2, 1, 3))
        dq = (dot(ds, k, NN) * INV).astype(jnp.bfloat16)
        for i, at in enumerate(heads):
            dq_out[b, :, at] = dq[i * BLOCK : (i + 1) * BLOCK]
        if last:
            return
        dv_acc[group, :, window] += dot(gs_buf[...], p_buf[...], TN)
        dk_acc[group, :, window] += dot(q, ds_buf[...], TN)

        @pl.when(index == HEADS - 1)
        def _():
            for which in (1, 0):
                send_parts(which, 0, (0,))

        @pl.when(index == HEADS)
        def _():
            for which in (1, 0):
                send_parts(which, 0, (1, 2, 3))

        return 0

    lax.fori_loop(0, KV * HEADS - 1, unit, 0)
    send_parts(1, 1, (0,))
    send_parts(0, 1, (0,))
    unit(KV * HEADS - 1, 0, last=True)

    for group in range(KV):
        for which in range(2):
            for piece in range(len(PIECES)):
                part_copy(which, group, piece).wait_recv()
        lanes = slice(group * DH, (group + 1) * DH)
        for which, acc, out in ((0, dk_acc, dk_out), (1, dv_acc, dv_out)):
            for block in range(SHARD):
                at = slice(block * BLOCK, (block + 1) * BLOCK)
                total = acc[group, :, (12 + block) * BLOCK : (13 + block) * BLOCK]
                if which == 0:
                    total = total * INV
                for delta in (1, 2, 3):
                    if delta < 3 or block > 0:
                        total = total + landed[which, group, delta - 1, :, at].astype(jnp.float32)
                out[at, lanes] = total.T.astype(jnp.bfloat16)

    for step in range(1, HEADS):
        for which in range(2):
            kv_copy(which, step).wait_send()
            for group in range(KV):
                qg_copy(which, group, step).wait_send()
    for step in range(HEADS):
        to_second(step).wait_send()

        @pl.when(h != step)
        def _():
            pass_third(step).wait_send()

        to_sibling(step).wait_send()

    for group in range(KV):
        for which in range(2):
            for piece in range(len(PIECES)):
                part_copy(which, group, piece).wait_send()


def shards(queries, key_states, value_states, out_grads, doc_blocks):
    bf16, f32 = jnp.bfloat16, jnp.float32
    anywhere = pl.BlockSpec(memory_space=pl.ANY)
    vmem = pl.BlockSpec(memory_space=pltpu.VMEM)
    dma = pltpu.SemaphoreType.DMA
    tokens = SHARD * BLOCK
    out, dq, dk, dv = pl.pallas_call(
        kernel,
        out_shape=[
            pltpu.VMEM((SHARD, BLOCK, KV * QCOLS), bf16),
            pltpu.VMEM((SHARD, BLOCK, KV * QCOLS), bf16),
            pltpu.VMEM((tokens, KV * DH), bf16),
            pltpu.VMEM((tokens, KV * DH), bf16),
        ],
        in_specs=[pl.BlockSpec(memory_space=pltpu.SMEM)] + [anywhere] * 4,
        out_specs=[vmem] * 4,
        scratch_shapes=[
            pltpu.VMEM((SHARD, BLOCK, KV * QCOLS), bf16),
            pltpu.VMEM((SHARD, BLOCK, KV * QCOLS), bf16),
            pltpu.VMEM((2, SLOTS * BLOCK, KV * DH), bf16),
            pltpu.VMEM((KV, DH, SLOTS * BLOCK), f32),
            pltpu.VMEM((KV, DH, SLOTS * BLOCK), f32),
            pltpu.VMEM((2, KV, DH, 12 * BLOCK), bf16),
            pltpu.VMEM((2, KV, 3, DH, tokens), bf16),
            pltpu.VMEM((QCOLS, SPAN), bf16),
            pltpu.VMEM((QCOLS, SPAN), bf16),
            pltpu.VMEM((QCOLS, DH), bf16),
            dma((2, HEADS)), dma((2, HEADS)),
            dma((3, HEADS)), dma((3, HEADS)),
            dma((2, KV, HEADS)), dma((2, KV, HEADS)),
            dma((2, KV, 4)), dma((2, KV, 4)),
        ],
        compiler_params=pltpu.CompilerParams(
            collective_id=0, has_side_effects=True, vmem_limit_bytes=58 * 2**20
        ),
        name="attention",
    )(doc_blocks, queries, key_states, value_states, out_grads)
    width = KV * QCOLS
    return out.reshape(tokens, width), dq.reshape(tokens, width), dk, dv


def solution(mesh):
    entry = P(("ctx", "head"), None)
    return jax.shard_map(
        shards,
        mesh=mesh,
        in_specs=(entry, entry, entry, entry, P()),
        out_specs=(P("ctx", "head"),) * 4,
        check_vma=False,
    )
```
